256 devices in a mesh: dp: 16 (over z_lo, y), fsdp: 16 (over z_hi, x, core).
Axes of the slice: x: 4, y: 4, z: 8 (z_hi: 2, z_lo: 4; z = z_hi * 4 + z_lo), core: 2. Of those that a mesh axis runs over, the one named last changes fastest.
Arguments:
- views: float32 [1536, 64, 256], P('fsdp', 'dp'), may hold values from -90 to 90
- view_moves: int32 [16, 2], replicated, may hold values from 0 to 1, as said below
- grad_out: float32 [1536, 32, 256], P('fsdp', 'dp'), may hold values from -6 to 6
- kernel: float32 [1536, 49], P('fsdp'), may hold values from -0.875 to 0.875
- norm_gain: float32 [1536], P('fsdp'), may hold values from 0.25 to 1.75
- w_up: float32 [1536, 6144], P(None, 'fsdp'), may hold values from -0.15625 to 0.15625
- bias_up: float32 [6144], P('fsdp'), may hold values from -3 to 3
- w_down: float32 [6144, 1536], P('fsdp'), may hold values from -0.078125 to 0.078125
- layer_scale: float32 [1536], P('fsdp'), may hold values from 0.5 to 1.5
Outputs:
- mixed: float32 [1536, 32, 256], P('fsdp', 'dp')
- grad_views: float32 [1536, 64, 256], P('fsdp', 'dp')
- grad_kernel: float32 [1536, 49], P('fsdp')
- grad_gain: float32 [1536], P('fsdp')
- grad_up: float32 [1536, 6144], P(None, 'fsdp')
- grad_bias_up: float32 [6144], P('fsdp')
- grad_down: float32 [6144, 1536], P('fsdp')
- grad_scale: float32 [1536], P('fsdp')
The draws below stay inside these ranges and needn't reach their ends.
Inputs may be any that keep to these rules, and one draw needn't show every extreme that they name: view_moves[g,0] views leave group g for group g-1 and view_moves[g,1] for group g+1; the first group sends none to a lower group and the last none to a higher one; the live counts of the first step lie between 0 and 4, 4 in some group, and every group ends with exactly 2 views.
All inputs are finite; a program needn't handle non-finite values.
Results may differ from the reference program's by a relative error of at most 0.00013.
Values sent between devices are 32-bit elements; how exact they have to be, the bound alone decides.
No kernel may reach another device: no remote copies, remote signals or barrier semaphores. Data moves between devices by JAX's collectives and lax.ppermute only.
A program may use at most 128 MiB of HBM per device.

```python
import jax
import jax.numpy as jnp
from jax import lax

C = 1536
HID = 6144
SIDE = 16
KS = 7
VG = 2
CAP = 1
SLOTS = 4
PIX = 256
GROUPS = 16
VIEWS = 32


def draw_views(key, part):
    key = jax.random.fold_in(key, 5)
    subkeys = jax.random.split(key, 3)
    channel_rise = 10.0 ** (jnp.arange(C, dtype=jnp.float32) / C)
    channel_spread = jnp.exp(jax.random.uniform(subkeys[0], (C,), jnp.float32, jnp.log(0.6), jnp.log(1.6)))
    pixel_spread = jnp.exp(jax.random.uniform(subkeys[1], (1, GROUPS * SLOTS, PIX), jnp.float32, jnp.log(0.3), jnp.log(3.0)))
    scales = 0.3 * (channel_rise * channel_spread)[:, None, None] * pixel_spread
    fluctuation = jnp.clip(jax.random.normal(subkeys[2], (C, GROUPS * SLOTS, PIX), jnp.float32), -6.0, 6.0)
    return fluctuation * scales


def draw_view_moves(key, part):
    key = jax.random.fold_in(key, 9)
    subkeys = jax.random.split(key, 2)
    counts = jax.random.randint(subkeys[0], (GROUPS, 2), 0, CAP + 1)
    busiest = jax.random.randint(subkeys[1], (), 1, GROUPS - 1)
    group_ids = jnp.arange(GROUPS, dtype=jnp.int32)
    to_left = counts[:, 0]
    to_right = counts[:, 1]
    to_left = jnp.where(group_ids == busiest, CAP, to_left)
    to_right = jnp.where(group_ids == busiest, CAP, to_right)
    to_right = jnp.where(group_ids == busiest - 1, 0, to_right)
    to_left = jnp.where(group_ids == busiest + 1, 0, to_left)
    to_right = jnp.where(group_ids == GROUPS - 2, CAP, to_right)
    to_left = jnp.where(group_ids == 0, 0, to_left)
    to_right = jnp.where(group_ids == GROUPS - 1, 0, to_right)
    return jnp.stack([to_left, to_right], axis=1).astype(jnp.int32)


def steps_of(own_key, extent, shards, smallest, top_value):
    def one(dim, blocks):
        draws = jax.random.uniform(jax.random.fold_in(jax.random.fold_in(own_key, 6), dim), (blocks,), jnp.float32, smallest / len(shards), top_value / len(shards))
        return jnp.repeat(jnp.exp(draws), extent[dim] // blocks).reshape((-1,) + (1,) * (len(extent) - dim - 1))

    loudness = one(*shards[0])
    for cut in shards[1:]:
        loudness = loudness * one(*cut)
    return loudness


def bell_draw(key, dims, deviation, most, shards=(), held_as=jnp.bfloat16):
    array = jax.random.normal(key, dims, jnp.float32) * deviation
    if len(shards) > 0:
        array = steps_of(key, dims, shards, -0.22, 0.18) * array
    return jnp.clip(array, min=-most, max=most).astype(held_as)


def setup_inputs(seed: int = 0) -> dict:
    arg_keys = jax.random.split(jax.random.key(seed), 10)
    views = draw_views(jax.random.fold_in(arg_keys[9], 71), 0)
    view_moves = draw_view_moves(jax.random.fold_in(arg_keys[9], 71), 0)
    grad_out = bell_draw(arg_keys[2], (C, VIEWS, PIX), 1.0, 6.0, ((0, 16), (1, 16)), jnp.float32)
    kernel = bell_draw(arg_keys[3], (C, KS * KS), (KS * KS) ** -0.5, 0.875, ((0, 16),), jnp.float32)
    norm_gain = jnp.clip(1.0 + 0.15 * jax.random.normal(arg_keys[4], (C,), jnp.float32), 0.25, 1.75)
    w_up = bell_draw(arg_keys[5], (C, HID), C ** -0.5, 0.15625, ((1, 16),), jnp.float32)
    bias_up = bell_draw(arg_keys[6], (HID,), 0.5, 3.0, ((0, 16),), jnp.float32)
    w_down = bell_draw(arg_keys[7], (HID, C), HID ** -0.5, 0.078125, ((0, 16),), jnp.float32)
    layer_scale = jnp.clip(0.5 + 1.0 * jax.random.uniform(arg_keys[8], (C,), jnp.float32) ** steps_of(arg_keys[8], (C,), ((0, 16),), -0.2, 0.2), 0.5, 1.5)
    return dict(views=views, view_moves=view_moves, grad_out=grad_out, kernel=kernel, norm_gain=norm_gain, w_up=w_up, bias_up=bias_up, w_down=w_down, layer_scale=layer_scale)


EPSILON = 1e-06
PRECISE = lax.Precision.HIGHEST

def depthwise(maps, kernel):
    channels, count = (maps.shape[0], maps.shape[1])
    reach = KS // 2
    grid = maps.reshape(channels, count, SIDE, SIDE)
    padded = jnp.pad(grid, ((0, 0), (0, 0), (reach, reach), (reach, reach)))
    total = jnp.zeros_like(grid)
    for shift_row in range(KS):
        for shift_col in range(KS):
            weight = kernel[:, shift_row * KS + shift_col][:, None, None, None]
            total = total + weight * padded[:, :, shift_row:shift_row + SIDE, shift_col:shift_col + SIDE]
    return total.reshape(channels, count, SIDE * SIDE)

def block_forward(placed, kernel, norm_gain, w_up, bias_up, w_down, layer_scale):
    conv_out = depthwise(placed, kernel)
    centre = lax.optimization_barrier(jnp.mean(conv_out, axis=0))
    spread = lax.optimization_barrier(jnp.mean((conv_out - centre) ** 2, axis=0))
    standard = (conv_out - centre) * lax.rsqrt(spread + EPSILON)
    normed = standard * norm_gain[:, None, None]
    pre_act = jnp.einsum('cvp,ch->vph', normed, w_up, precision=PRECISE) + bias_up
    hidden = jax.nn.gelu(pre_act, approximate=False)
    branch = jnp.einsum('vph,hc->cvp', hidden, w_down, precision=PRECISE)
    return placed + layer_scale[:, None, None] * branch

def route_index(view_moves):
    to_left = view_moves[:, 0]
    to_right = view_moves[:, 1]
    empty_one = jnp.zeros((1,), jnp.int32)
    from_left = jnp.concatenate([empty_one, to_right[:-1]])
    from_right = jnp.concatenate([to_left[1:], empty_one])
    live_counts = VG + to_left + to_right - from_left - from_right
    kept_count = live_counts - to_left - to_right
    prior_live = jnp.concatenate([empty_one, live_counts[:-1]])
    group_col = jnp.arange(GROUPS, dtype=jnp.int32)[:, None]
    position = jnp.arange(VG, dtype=jnp.int32)[None, :]
    arrive = from_left[:, None]
    kept_col = kept_count[:, None]
    source_left = (group_col - 1) * SLOTS + prior_live[:, None] - arrive + position
    source_own = group_col * SLOTS + to_left[:, None] + position - arrive
    source_right = (group_col + 1) * SLOTS + position - arrive - kept_col
    source = jnp.where(position < arrive, source_left, jnp.where(position < arrive + kept_col, source_own, source_right))
    return source.reshape(-1).astype(jnp.int32)

def reference(views, view_moves, grad_out, kernel, norm_gain, w_up, bias_up, w_down, layer_scale):
    source = route_index(view_moves)
    placed = jnp.take(views, source, axis=1)
    channels = placed.shape[0]
    group_blocks = placed.reshape(channels, GROUPS, VG, PIX).transpose(1, 0, 2, 3)
    cot_blocks = grad_out.reshape(channels, GROUPS, VG, PIX).transpose(1, 0, 2, 3)
    weights = (kernel, norm_gain, w_up, bias_up, w_down, layer_scale)

    def scan_step(totals, inputs_pair):
        group_block, cot_block = inputs_pair
        result, pullback = jax.vjp(block_forward, group_block, *weights)
        gradients = pullback(cot_block)
        totals = tuple((total_now + term for total_now, term in zip(totals, gradients[1:])))
        return (totals, (result, gradients[0]))
    initial = tuple((jnp.zeros_like(weight) for weight in weights))
    totals, (results, grad_blocks) = lax.scan(scan_step, initial, (group_blocks, cot_blocks))
    mixed = results.transpose(1, 0, 2, 3).reshape(channels, VIEWS, PIX)
    grad_placed = grad_blocks.transpose(1, 0, 2, 3).reshape(channels, VIEWS, PIX)
    grad_views = jnp.zeros_like(views).at[:, source].set(grad_placed)
    return (mixed, grad_views, totals[0], totals[1], totals[2], totals[3], totals[4], totals[5])
```

```python
import jax
import jax.numpy as jnp
from jax import lax
from jax.sharding import PartitionSpec as P

C = 1536
SIDE = 16
KS = 7
VG = 2
CAP = 1
PIX = SIDE * SIDE
FS = 16
BLK = C // FS

EPSILON = 1e-06
PRECISE = lax.Precision.HIGH
ROOT_HALF = 0.7071067811865476
GAUSS_NORM = 0.3989422804014327

ORDER = [0, 8, 2, 10, 4, 12, 6, 14, 1, 9, 3, 11, 5, 13, 7, 15]


def swap(value, axis, mask):
    count = lax.axis_size(axis)
    return lax.ppermute(value, axis, [(i, i ^ mask) for i in range(count)])


def shifted(value, axis, steps):
    count = lax.axis_size(axis)
    leading, last = (max(0, -steps), min(count, count - steps))
    return lax.ppermute(value, axis, [(source, source + steps) for source in range(leading, last)])


def gather_blocks(block):
    pair = jnp.concatenate([block, swap(block, "fsdp", 8)], axis=0)
    parts = [pair] + [swap(pair, "fsdp", 2 * k) for k in (1, 2, 3)]
    return jnp.concatenate(parts + [swap(part, "fsdp", 1) for part in parts], axis=0)


def scatter_blocks(mine, other):
    rows = mine.shape[0] // 4
    half = mine + swap(other, "fsdp", 1)
    pair = half[:rows]
    for k in (1, 2, 3):
        pair = pair + swap(half[rows * k : rows * (k + 1)], "fsdp", 2 * k)
    return pair[: rows // 2] + swap(pair[rows // 2 :], "fsdp", 8)


def sum_small(value, axis, stages):
    for masks in stages:
        value = sum((swap(value, axis, mask) for mask in masks), value)
    return value


def row_slice(value, index, rows):
    return lax.dynamic_slice_in_dim(value, index * rows, rows, 0)


def sum_groups(grad):
    place = lax.axis_index("dp")
    along_y, along_z = place % 4, place // 4
    rows = grad.shape[0] // 4
    piece = row_slice(grad, along_y, rows)
    for k in (1, 2, 3):
        piece = piece + swap(row_slice(grad, along_y ^ k, rows), "dp", k)
    small = rows // 4
    own = row_slice(piece, along_z, small)
    for k in (1, 2, 3):
        own = own + swap(row_slice(piece, along_z ^ k, small), "dp", 4 * k)
    piece = jnp.zeros_like(piece)
    for k in range(4):
        got = own if k == 0 else swap(own, "dp", 4 * k)
        piece = lax.dynamic_update_slice_in_dim(piece, got, (along_z ^ k) * small, 0)
    total = jnp.zeros_like(grad)
    for k in range(4):
        got = piece if k == 0 else swap(piece, "dp", k)
        total = lax.dynamic_update_slice_in_dim(total, got, (along_y ^ k) * rows, 0)
    return total


def to_arrival(value):
    me = lax.axis_index("fsdp")
    return jnp.concatenate([row_slice(value, me ^ m, BLK) for m in ORDER], axis=0)


def from_arrival(value):
    me = lax.axis_index("fsdp")
    out = jnp.zeros_like(value)
    for b, m in enumerate(ORDER):
        out = lax.dynamic_update_slice_in_dim(out, value[b * BLK : (b + 1) * BLK], (me ^ m) * BLK, 0)
    return out


def depthwise(maps, kernel):
    channels, count = (maps.shape[0], maps.shape[1])
    reach = KS // 2
    grid = maps.reshape(channels, count, SIDE, SIDE)
    padded = jnp.pad(grid, ((0, 0), (0, 0), (reach, reach), (reach, reach)))
    total = jnp.zeros_like(grid)
    for shift_row in range(KS):
        for shift_col in range(KS):
            weight = kernel[:, shift_row * KS + shift_col][:, None, None, None]
            total = (
                total
                + weight * padded[:, :, shift_row : shift_row + SIDE, shift_col : shift_col + SIDE]
            )
    return total.reshape(channels, count, PIX)


def depthwise_back(placed, delta, kernel):
    channels, count = (placed.shape[0], placed.shape[1])
    reach = KS // 2
    pad_spec = ((0, 0), (0, 0), (reach, reach), (reach, reach))
    padded_in = jnp.pad(placed.reshape(channels, count, SIDE, SIDE), pad_spec)
    grid_delta = delta.reshape(channels, count, SIDE, SIDE)
    padded_delta = jnp.pad(grid_delta, pad_spec)
    columns = []
    through = jnp.zeros_like(grid_delta)
    for shift_row in range(KS):
        for shift_col in range(KS):
            window = padded_in[:, :, shift_row : shift_row + SIDE, shift_col : shift_col + SIDE]
            columns.append(jnp.sum(grid_delta * window, axis=(1, 2, 3)))
            mirror_row = KS - 1 - shift_row
            mirror_col = KS - 1 - shift_col
            weight = kernel[:, shift_row * KS + shift_col][:, None, None, None]
            through = (
                through
                + weight
                * padded_delta[:, :, mirror_row : mirror_row + SIDE, mirror_col : mirror_col + SIDE]
            )
    return (jnp.stack(columns, axis=1), through.reshape(channels, count, PIX))


def shards(views, view_moves, grad_out, kernel, norm_gain, w_up, bias_up, w_down, layer_scale):
    channels, slots, pixels = views.shape
    hid = w_up.shape[1]
    spots = VG * pixels
    group_now = lax.axis_index("dp")
    to_left = view_moves[:, 0]
    to_right = view_moves[:, 1]
    none = jnp.zeros((1,), jnp.int32)
    from_left = jnp.concatenate([none, to_right[:-1]])
    from_right = jnp.concatenate([to_left[1:], none])
    mine = jnp.arange(view_moves.shape[0], dtype=jnp.int32) == group_now
    my_left = jnp.sum(jnp.where(mine, to_left, 0))
    my_right = jnp.sum(jnp.where(mine, to_right, 0))
    arrive_left = jnp.sum(jnp.where(mine, from_left, 0))
    arrive_right = jnp.sum(jnp.where(mine, from_right, 0))
    my_live = VG + my_left + my_right - arrive_left - arrive_right
    kept_count = my_live - my_left - my_right

    scale_col = layer_scale[:, None]
    cot = grad_out.reshape(channels, spots)
    scot = gather_blocks(cot * scale_col)
    gain = gather_blocks(norm_gain[None, :])[:, :, None].reshape(C, 1)

    tail = lax.dynamic_slice_in_dim(views, jnp.maximum(my_live - 1, 0), 1, 1)
    next_views = shifted(views[:, :1], "dp", -1)
    prior_views = shifted(tail, "dp", 1)
    candidates = jnp.concatenate([prior_views, views, next_views], axis=1)
    sources = []
    for j in range(VG):
        sources.append(
            jnp.where(
                j < arrive_left,
                CAP - arrive_left + j,
                jnp.where(
                    j < arrive_left + kept_count,
                    CAP + my_left + j - arrive_left,
                    CAP + slots + j - arrive_left - kept_count,
                ),
            )
        )
    placed = jnp.concatenate(
        [lax.dynamic_slice_in_dim(candidates, s, 1, 1) for s in sources], axis=1
    )
    conv_own = depthwise(placed, kernel).reshape(channels, spots)
    conv_all = gather_blocks(conv_own)
    w_up_a = to_arrival(w_up)
    w_down_a = to_arrival(w_down.T)
    d_hidden = jnp.einsum("ch,cp->hp", w_down_a, scot, precision=PRECISE)
    gain_up = jnp.einsum("co,ch->oh", gain, w_up_a, precision=lax.Precision.HIGHEST)

    centre = jnp.mean(conv_all, axis=0)
    spread = jnp.mean((conv_all - centre) ** 2, axis=0)
    inv_std = lax.rsqrt(spread + EPSILON)
    normed = (conv_all - centre) * inv_std * gain
    up = jnp.einsum("ch,cp->hp", w_up_a, normed, precision=PRECISE)
    pre_act = up + bias_up[:, None]
    phi_cum = 0.5 * (1.0 + lax.erf(pre_act * ROOT_HALF))
    hidden = pre_act * phi_cum
    slope = phi_cum + pre_act * jnp.exp(-0.5 * pre_act * pre_act) * GAUSS_NORM
    d_pre = d_hidden * slope
    grad_down_a = jnp.einsum("cp,hp->ch", scot, hidden, precision=PRECISE)
    grad_up_a = jnp.einsum("cp,hp->ch", normed, d_pre, precision=PRECISE)
    half = C // 2
    dn_other = jnp.einsum("ch,hp->cp", w_up_a[half:], d_pre, precision=PRECISE)
    dn_mine = jnp.einsum("ch,hp->cp", w_up_a[:half], d_pre, precision=PRECISE)
    br_other = jnp.einsum("ch,hp->cp", w_down_a[half:], hidden, precision=PRECISE)
    br_mine = jnp.einsum("ch,hp->cp", w_down_a[:half], hidden, precision=PRECISE)
    sums = jnp.stack([jnp.sum(d_pre * gain_up.T, axis=0), jnp.sum(d_pre * up, axis=0)])
    sums = sum_small(sums, "fsdp", ((1,), (2, 4, 6), (8,)))
    grad_bias = jnp.sum(d_pre, axis=1)

    d_normed = scatter_blocks(dn_mine, dn_other)
    grad_down = from_arrival(sum_groups(grad_down_a)).T
    branch = scatter_blocks(br_mine, br_other)
    grad_up = from_arrival(sum_groups(grad_up_a))

    standard = (conv_own - centre) * inv_std
    mixed = placed + (scale_col * branch).reshape(channels, VG, pixels)
    grad_scale = jnp.sum(cot * branch, axis=1)
    grad_gain = jnp.sum(d_normed * standard, axis=1)
    d_conv = inv_std * (d_normed * norm_gain[:, None] - sums[0] / C - standard * (sums[1] / C))
    grad_kernel, through = depthwise_back(placed, d_conv.reshape(channels, VG, pixels), kernel)
    d_placed = grad_out + through

    small = jnp.concatenate([grad_kernel.reshape(-1), grad_gain, grad_bias, grad_scale])
    count = small.shape[0]
    small = jnp.pad(small, (0, -count % 1024)).reshape(-1, 128)
    small = sum_small(small, "dp", ((1, 2, 3), (4, 8, 12))).reshape(-1)
    taps = KS * KS * channels
    grad_kernel = small[:taps].reshape(channels, KS * KS)
    grad_gain = small[taps : taps + channels]
    grad_bias = small[taps + channels : taps + channels + hid]
    grad_scale = small[taps + channels + hid : taps + 2 * channels + hid]

    to_below = jnp.where(arrive_left > 0, d_placed[:, :1], 0.0)
    to_above = jnp.where(arrive_right > 0, d_placed[:, VG - 1 :], 0.0)
    from_above = shifted(to_below, "dp", -1)
    from_below = shifted(to_above, "dp", 1)
    slot_ids = jnp.arange(slots, dtype=jnp.int32)[None, :, None]
    grad_views = jnp.zeros_like(views)
    for j in range(VG):
        grad_views = grad_views + jnp.where(
            slot_ids == sources[j] - CAP, d_placed[:, j : j + 1], 0.0
        )
    grad_views = jnp.where((slot_ids == 0) & (my_left > 0), from_below, grad_views)
    grad_views = jnp.where((slot_ids == my_live - 1) & (my_right > 0), from_above, grad_views)
    return (mixed, grad_views, grad_kernel, grad_gain, grad_up, grad_bias, grad_down, grad_scale)


def solution(mesh):
    return jax.shard_map(
        shards,
        mesh=mesh,
        in_specs=(
            P("fsdp", "dp", None),
            P(),
            P("fsdp", "dp", None),
            P("fsdp", None),
            P("fsdp"),
            P(None, "fsdp"),
            P("fsdp"),
            P("fsdp", None),
            P("fsdp"),
        ),
        out_specs=(
            P("fsdp", "dp", None),
            P("fsdp", "dp", None),
            P("fsdp", None),
            P("fsdp"),
            P(None, "fsdp"),
            P("fsdp"),
            P("fsdp", None),
            P("fsdp"),
        ),
        check_vma=False,
    )
```

```python
import functools

import jax
import jax.numpy as jnp
from jax import lax
from jax.experimental import pallas as pl
from jax.experimental.pallas import tpu as pltpu
from jax.sharding import PartitionSpec as P

C = 1536
HID = 384
SIDE = 16
KS = 7
REACH = KS // 2
VG = 2
CAP = 1
SLOTS = 4
PIX = SIDE * SIDE
SPOTS = VG * PIX
BLK = 96
EXT = 8
GROUPS = 16

EPSILON = 1e-06
ROOT_HALF = 0.7071067811865476
GAUSS_NORM = 0.3989422804014327
F32 = jnp.float32
BF16 = jnp.bfloat16

NEAR = ((0, 2), (6, 4))
FAR = ((8, 14), (10, 12))
GROUPED = NEAR + FAR + tuple((a ^ 1, b ^ 1) for a, b in NEAR + FAR)
SCATTER = {first: (0, 8, 8 - first, 16 - first, first, 8 + first, 4, 12) for first in (2, 6)}


def call(body, outs, ins, scratch=(), smem=(), after=None, us=1):
    after = [] if after is None else list(after) if isinstance(after, tuple) else [after]
    count = len(ins)
    if after:
        inner = body
        body = lambda *refs: inner(*refs[:count], *refs[count + len(after) :])
        ins = list(ins) + after
    shapes = [jax.ShapeDtypeStruct(s, d) for s, d in outs]
    spec = pl.BlockSpec(memory_space=pltpu.VMEM)
    return pl.pallas_call(
        body,
        out_shape=shapes,
        in_specs=[
            pl.BlockSpec(memory_space=pltpu.SMEM)
            if i in smem
            else pl.BlockSpec(memory_space=pl.ANY)
            if i >= count
            else spec
            for i in range(len(ins))
        ],
        out_specs=[spec] * len(outs),
        scratch_shapes=list(scratch),
        compiler_params=pltpu.CompilerParams(vmem_limit_bytes=40 * 2**20),
        cost_estimate=pl.CostEstimate(flops=us * 10**10, bytes_accessed=1024, transcendentals=0),
    )(*ins)


def swap(value, axis, mask):
    count = lax.axis_size(axis)
    return lax.ppermute(value, axis, [(i, i ^ mask) for i in range(count)])


def shifted(value, axis, steps):
    count = lax.axis_size(axis)
    leading, last = (max(0, -steps), min(count, count - steps))
    return lax.ppermute(value, axis, [(source, source + steps) for source in range(leading, last)])


def halves(value):
    high = value.astype(BF16)
    return high, (value - high.astype(F32)).astype(BF16)


def split_rows(source, high, low, first, count, target, chunk=32):
    def step(i, _):
        take = pl.ds(pl.multiple_of(first + i * chunk, chunk), chunk)
        put = pl.ds(pl.multiple_of(target + i * chunk, chunk), chunk)
        high[put, :], low[put, :] = halves(source[take, :])
        return 0

    lax.fori_loop(0, count // chunk, step, 0)


def product(a_high, a_low, b_high, b_low, contract):
    dims = (contract, ((), ()))
    dot = functools.partial(lax.dot_general, dimension_numbers=dims, preferred_element_type=F32)
    return dot(a_high, b_high) + dot(a_high, b_low) + dot(a_low, b_high)


NN = ((1,), (0,))
NT = ((1,), (1,))


def as_column(row):
    at = lax.broadcasted_iota(jnp.int32, (BLK, BLK), 0)
    to = lax.broadcasted_iota(jnp.int32, (BLK, BLK), 1)
    return jnp.sum(jnp.where(at == to, jnp.broadcast_to(row, (BLK, BLK)), 0.0), axis=1, keepdims=True)


def start_body(moves, views, head, tail, picks):
    g = lax.axis_index("dp")
    below = jnp.maximum(g - 1, 0)
    above = jnp.minimum(g + 1, GROUPS - 1)
    to_left = moves[g, 0]
    to_right = moves[g, 1]
    from_left = jnp.where(g > 0, moves[below, 1], 0)
    from_right = jnp.where(g < GROUPS - 1, moves[above, 0], 0)
    live = VG + to_left + to_right - from_left - from_right
    kept = live - to_left - to_right
    for j in range(VG):
        picks[j] = jnp.where(
            j < from_left,
            CAP - from_left + j,
            jnp.where(
                j < from_left + kept,
                CAP + to_left + j - from_left,
                CAP + SLOTS + j - from_left - kept,
            ),
        )
    picks[2] = live
    picks[3] = to_left
    picks[4] = to_right
    picks[5] = from_left
    picks[6] = from_right
    picks[7] = 0
    head[...] = views[:, 0, :]
    for s in range(SLOTS):

        @pl.when(jnp.maximum(live - 1, 0) == s)
        def _(s=s):
            tail[...] = views[:, s, :]


def scaled_body(cot, scale, gain, scot):
    column = as_column(scale[...])
    for v in range(VG):
        scot[0:BLK, v * PIX : (v + 1) * PIX] = cot[:, v, :] * column
    scot[BLK : BLK + EXT, :] = jnp.zeros((EXT, SPOTS), F32)
    scot[BLK : BLK + 1, 0:BLK] = gain[...]


def lane_place():
    lane = lax.broadcasted_iota(jnp.int32, (8, PIX), 1)
    return lane // SIDE, lane % SIDE


def moved(value, by, unit, where):
    if by == 0:
        return value
    rolled = pltpu.roll(value, (-by * unit) % PIX, 1)
    inside = (where + by >= 0) & (where + by < SIDE)
    return jnp.where(inside, rolled, 0.0)


def forward_body(picks, views, prior, after, kernel, placed, conv):
    def one(j, pick):
        spot = slice(j * PIX, (j + 1) * PIX)

        @pl.when(pick == 0)
        def _():
            placed[:, spot] = prior[...]

        @pl.when(pick == SLOTS + 1)
        def _():
            placed[:, spot] = after[...]

        for s in range(SLOTS):

            @pl.when(pick == CAP + s)
            def _(s=s):
                placed[:, spot] = views[:, s, :]

    for j in range(VG):
        one(j, picks[j])
    row, col = lane_place()

    def step(i, _):
        at = pl.ds(pl.multiple_of(i * 8, 8), 8)
        taps = kernel[at, :]
        maps = [placed[at, v * PIX : (v + 1) * PIX] for v in range(VG)]
        total = [jnp.zeros((8, PIX), F32) for _ in range(VG)]
        wide = [[moved(m, b - REACH, 1, col) for b in range(KS)] for m in maps]
        for a in range(KS):
            weights = [jnp.broadcast_to(taps[:, a * KS + b : a * KS + b + 1], (8, PIX)) for b in range(KS)]
            for v in range(VG):
                line = weights[0] * wide[v][0]
                for b in range(1, KS):
                    line = line + weights[b] * wide[v][b]
                total[v] = total[v] + moved(line, a - REACH, SIDE, row)
        for v in range(VG):
            conv[at, v * PIX : (v + 1) * PIX] = total[v]
        return 0

    lax.fori_loop(0, BLK // 8, step, 0)


def first_weights_body(w_up, w_down, u_high, u_low, d_high, d_low, done):
    def step(i, _):
        at = pl.ds(pl.multiple_of(i * 128, 128), 128)
        u_high[:, at], u_low[:, at] = halves(w_up[at, :].T)
        return 0

    lax.fori_loop(0, C // 128, step, 0)
    split_rows(w_down, d_high, d_low, 0, HID, 0)
    done[...] = jnp.zeros((8, 128), F32)


def second_weights_body(w_up, w_down, u_high, u_low, d_high, d_low, done, turned):
    f = lax.axis_index("fsdp")

    def step(i, _):
        at = pl.ds(pl.multiple_of(i * 128, 128), 128)
        turned[at, :] = w_down[:, at].T
        return 0

    lax.fori_loop(0, C // 128, step, 0)
    for source, high, low, first in ((w_up, u_high, u_low, 6), (turned, d_high, d_low, 6)):
        order = SCATTER[first]
        for q, m in enumerate(order + tuple(m ^ 1 for m in order)):
            split_rows(source, high, low, (f ^ m) * BLK, BLK, q * BLK)
    done[...] = jnp.zeros((8, 128), F32)


def cot_body(*refs):
    parts, refs = refs[:8], refs[8:]
    d_high, d_low, u_high, u_low, s_high, s_low, gains, gain_up, d_hidden, g_high, g_low = refs
    f = lax.axis_index("fsdp")
    for part, masks in zip(parts, GROUPED):
        for q, m in enumerate(masks):
            first = q * (BLK + EXT)
            at = pl.ds(pl.multiple_of((f ^ m) * BLK, 32), BLK)
            s_high[at, :], s_low[at, :] = halves(part[first : first + BLK, :])
            column = as_column(part[first + BLK : first + BLK + 1, 0:BLK])
            gains[at, :] = jnp.broadcast_to(column, (BLK, 128))
    def tile(n, _):
        at = pl.ds(pl.multiple_of(n * 256, 256), 256)
        d_hidden[:, at] = product(d_high[...], d_low[...], s_high[:, at], s_low[:, at], NN)
        return 0

    lax.fori_loop(0, SPOTS // 256, tile, 0)
    split_rows(gains, g_high, g_low, 0, C, 0)
    gain_up[...] = product(u_high[...], u_low[...], g_high[...], g_low[...], NN)


def up_body(*refs):
    parts, refs = refs[:8], refs[8:]
    gains, u_high, u_low, bias, gain_up, s_high, s_low, d_hidden = refs[:8]
    keep, send_a, send_b, h_high, h_low, p_high, p_low, n_high, n_low, stats, sums, d_bias = refs[8:20]
    up, y_high, y_low = refs[20:]
    f = lax.axis_index("fsdp")
    y = lax.axis_index("dp") % 4
    centre = sum(jnp.sum(part[...], axis=0, keepdims=True) for part in parts) / C
    spread = sum(jnp.sum((part[...] - centre) ** 2, axis=0, keepdims=True) for part in parts) / C
    inv_std = lax.rsqrt(spread + EPSILON)
    stats[...] = jnp.zeros((EXT, SPOTS), F32)
    stats[0:1, :] = centre
    stats[1:2, :] = inv_std
    for part, masks in zip(parts, GROUPED):
        for q, m in enumerate(masks):

            def piece(i, _, part=part, q=q, m=m):
                take = pl.ds(pl.multiple_of(q * BLK + i * 32, 32), 32)
                put = pl.ds(pl.multiple_of((f ^ m) * BLK + i * 32, 32), 32)
                gain = gains[put, :]
                value = (part[take, :] - centre) * inv_std * jnp.concatenate([gain] * 4, axis=1)
                n_high[put, :], n_low[put, :] = halves(value)
                return 0

            lax.fori_loop(0, BLK // 32, piece, 0)

    def tile(n, _):
        at = pl.ds(pl.multiple_of(n * 256, 256), 256)
        up[:, at] = product(u_high[...], u_low[...], n_high[:, at], n_low[:, at], NN)
        return 0

    lax.fori_loop(0, SPOTS // 256, tile, 0)

    def gelu(i, total):
        at = pl.ds(pl.multiple_of(i * 32, 32), 32)
        raw = up[at, :]
        pre = raw + jnp.concatenate([bias[at, :]] * 4, axis=1)
        cum = 0.5 * (1.0 + lax.erf(pre * ROOT_HALF))
        hidden = pre * cum
        slope = cum + pre * jnp.exp(-0.5 * pre * pre) * GAUSS_NORM
        d_pre = d_hidden[at, :] * slope
        high, low = halves(hidden)
        h_high[at, :], h_low[at, :] = high, low
        put = pl.ds(pl.multiple_of(((i // 3) ^ y) * BLK + (i % 3) * 32, 32), 32)
        y_high[put, :], y_low[put, :] = high, low
        p_high[at, :], p_low[at, :] = halves(d_pre)
        d_bias[at, :] = jnp.broadcast_to(jnp.sum(d_pre, axis=1, keepdims=True), (32, 128))
        plain = jnp.sum(d_pre * jnp.concatenate([gain_up[at, :]] * 4, axis=1), axis=0, keepdims=True)
        cross = jnp.sum(d_pre * raw, axis=0, keepdims=True)
        return total[0] + plain, total[1] + cross

    zero = jnp.zeros((1, SPOTS), F32)
    plain, cross = lax.fori_loop(0, HID // 32, gelu, (zero, zero))
    sums[...] = jnp.zeros((EXT, SPOTS), F32)
    sums[0:1, :] = plain
    sums[1:2, :] = cross

    def down(n, _):
        at = pl.ds(pl.multiple_of(n * 256, 256), 256)
        got = product(y_high[...], y_low[...], s_high[at, :], s_low[at, :], NT)
        for k in range(4):
            lay_out(k, got[k * BLK : (k + 1) * BLK, :], keep, send_a, send_b, at)
        return 0

    lax.fori_loop(0, C // 256, down, 0)


def grad_up_body(n_high, n_low, p_high, p_low, keep, send_a, send_b):
    y = lax.axis_index("dp") % 4
    for k in range(4):
        at = pl.ds(pl.multiple_of((y ^ k) * HID, HID), HID)
        got = product(n_high[at, :], n_low[at, :], p_high[...], p_low[...], NT)
        lay_out(k, got, keep, send_a, send_b, slice(None))


def spread_body(a_high, a_low, b_high, b_low, sums, mine, other):
    for out, flip in ((other, 1), (mine, 0)):
        rows = slice(flip * 8 * BLK, (flip + 1) * 8 * BLK)

        def tile(n, _, out=out, rows=rows):
            at = pl.ds(pl.multiple_of(n * 256, 256), 256)
            high, low = a_high[rows, :], a_low[rows, :]
            out[0 : 8 * BLK, at] = product(high, low, b_high[:, at], b_low[:, at], NN)
            return 0

        lax.fori_loop(0, SPOTS // 256, tile, 0)
        out[8 * BLK : 8 * BLK + EXT, :] = sums[...]


def half_sum_body(a, b, keep, send):
    rows = keep.shape[0] - EXT
    sums = a[2 * rows :, :] + b[2 * rows :, :]
    for k, out in enumerate((keep, send)):
        at = slice(rows * k, rows * (k + 1))
        out[0:rows, :] = a[at, :] + b[at, :]
        out[rows : rows + EXT, :] = sums


def lay_out(k, value, keep, send_a, send_b, at):
    half = value.shape[0] // 2
    a_to, a_place = ((keep, 0), (send_a, 0), (send_a, 1), (keep, 1))[k]
    b_to, b_place = ((keep, 2), (keep, 3), (send_b, 1), (send_b, 0))[k]
    a_to[a_place * half : (a_place + 1) * half, at] = value[:half]
    b_to[b_place * half : (b_place + 1) * half, at] = value[half:]


def y_sum_body(keep, got_a, got_b, own, send_a, send_b):
    half = send_a.shape[0]
    one, two, three, four = (slice(half * i, half * (i + 1)) for i in range(4))
    own[one, :] = keep[one, :] + got_a[one, :]
    send_a[...] = keep[two, :] + got_a[two, :]
    own[two, :] = keep[three, :] + got_b[one, :]
    send_b[...] = keep[four, :] + got_b[two, :]


def z_cut_body(own, got_a, got_b, keep, send, piece):
    z = lax.axis_index("dp") // 4
    half = got_a.shape[0]
    rows = half // 2
    piece[:half, :] = own[:half, :] + got_a[...]
    piece[half:, :] = own[half:, :] + got_b[...]
    for out, pair in ((keep, (0, 2)), (send, (1, 3))):
        for i, q in enumerate(pair):
            out[i * rows : (i + 1) * rows, :] = piece[pl.ds(pl.multiple_of((z ^ q) * rows, 8), rows), :]


def z_sum_body(keep, got, own, send):
    rows = own.shape[0]
    own[...] = keep[:rows, :] + got[:rows, :]
    send[...] = keep[rows:, :] + got[rows:, :]


def z_join_body(pair, got, part_a, part_b, piece):
    z = lax.axis_index("dp") // 4
    half = part_a.shape[0]
    rows = half // 2
    for source, order in ((pair, (0, 2)), (got, (1, 3))):
        for i, q in enumerate(order):
            piece[pl.ds(pl.multiple_of((z ^ q) * rows, 8), rows), :] = source[i * rows : (i + 1) * rows, :]
    part_a[...] = piece[:half, :]
    part_b[...] = piece[half:, :]


def y_join_body(have_a, have_b, got_a, got_b, out):
    y = lax.axis_index("dp") % 4
    half = have_a.shape[0] // 2
    for source, which, order in ((have_a, 0, (0, 3)), (got_a, 0, (1, 2)), (have_b, 1, (0, 1)), (got_b, 1, (3, 2))):
        for i, k in enumerate(order):
            at = pl.ds(pl.multiple_of((y ^ k) * 2 * half + which * half, 8), half)
            out[at, :] = source[i * half : (i + 1) * half, :]


class GroupSum:
    def __init__(self, keep, send_a, send_b):
        self.half, self.columns = keep.shape[0] // 4, keep.shape[1]
        self.piece = [pltpu.VMEM((2 * self.half, self.columns), F32)]
        self.keep, self.send = keep, (send_a, send_b)

    def of(self, count):
        return ((count, self.columns), F32)

    def y_sum(self, after=None):
        ins = [self.keep, swap(self.send[0], "dp", 1), swap(self.send[1], "dp", 3)]
        outs = [self.of(2 * self.half), self.of(self.half), self.of(self.half)]
        self.keep, *self.send = call(y_sum_body, outs, ins, after=after)
        return self.keep

    def z_cut(self, after=None):
        ins = [self.keep, swap(self.send[0], "dp", 3), swap(self.send[1], "dp", 1)]
        outs = [self.of(self.half)] * 2
        self.keep, self.send = call(z_cut_body, outs, ins, scratch=self.piece, after=after)
        return self.keep

    def z_sum(self, after=None):
        ins = [self.keep, swap(self.send, "dp", 4)]
        outs = [self.of(self.half // 2)] * 2
        self.keep, self.send = call(z_sum_body, outs, ins, after=after)
        return self.keep

    def z_pair(self, after=None):
        own = self.keep + swap(self.send, "dp", 8)
        self.pair = pair_of(own, swap(own, "dp", 8), after)
        return self.pair

    def z_join(self, after=None):
        ins = [self.pair, swap(self.pair, "dp", 4)]
        outs = [self.of(self.half)] * 2
        self.parts = call(z_join_body, outs, ins, scratch=self.piece, after=after)
        return self.parts[0]

    def y_pair(self, after=None):
        one, two = self.parts
        ins = [one, swap(one, "dp", 3), two, swap(two, "dp", 1)]
        self.have = call(two_pairs_body, [self.of(2 * self.half)] * 2, ins, after=after)
        return self.have[1]

    def y_join(self, after=None):
        one, two = self.have
        ins = [one, two, swap(one, "dp", 1), swap(two, "dp", 3)]
        return call(y_join_body, [self.of(8 * self.half)], ins, after=after)[0]


def back_body(keep, got, stats, conv, placed, cot, kernel, gain, d_placed, small):
    centre, inv_std = stats[0:1, :], stats[1:2, :]
    mean_q = (keep[BLK : BLK + 1, :] + got[BLK : BLK + 1, :]) / C
    cross = slice(BLK + 1, BLK + 2)
    mean_cross = (keep[cross, :] + got[cross, :]) / C
    small[...] = jnp.broadcast_to(as_column(gain[...]), (BLK, 128))
    row, col = lane_place()
    lane = lax.broadcasted_iota(jnp.int32, (8, 128), 1)

    def step(i, _):
        at = pl.ds(pl.multiple_of(i * 8, 8), 8)
        taps = kernel[at, :]
        d_normed = keep[at, :] + got[at, :]
        standard = (conv[at, :] - centre) * inv_std
        gains = jnp.concatenate([small[at, :]] * 4, axis=1)
        d_conv = inv_std * (d_normed * gains - mean_q - standard * mean_cross)
        packed = jnp.where(
            lane == KS * KS, jnp.sum(d_normed * standard, axis=1, keepdims=True), 0.0
        )
        partial = {}
        for v in range(VG):
            spot = slice(v * PIX, (v + 1) * PIX)
            delta = d_conv[:, spot]
            maps = placed[at, spot]
            wide_d = [moved(delta, REACH - b, 1, col) for b in range(KS)]
            wide_x = [moved(maps, b - REACH, 1, col) for b in range(KS)]
            total = cot[at, v, :]
            for a in range(KS):
                line = jnp.zeros((8, PIX), F32)
                tall = moved(delta, REACH - a, SIDE, row)
                for b in range(KS):
                    t = a * KS + b
                    line = line + taps[:, t : t + 1] * wide_d[b]
                    term = tall * wide_x[b]
                    term = term[:, :128] + term[:, 128:]
                    partial[t] = term if v == 0 else partial[t] + term
                total = total + moved(line, REACH - a, SIDE, row)
            d_placed[v, at, :] = total
        for t in range(KS * KS):
            packed = jnp.where(lane == t, jnp.sum(partial[t], axis=1, keepdims=True), packed)
        small[at, :] = packed
        return 0

    lax.fori_loop(0, BLK // 8, step, 0)


def mixed_body(keep, got, placed, cot, scale, small_in, mixed, small):
    column = as_column(scale[...])
    lane = lax.broadcasted_iota(jnp.int32, (BLK, 128), 1)
    scale_sum = jnp.zeros((BLK, 1), F32)
    for v in range(VG):
        spot = slice(v * PIX, (v + 1) * PIX)
        branch = keep[0:BLK, spot] + got[0:BLK, spot]
        mixed[:, v, :] = placed[:, spot] + column * branch
        scale_sum = scale_sum + jnp.sum(cot[:, v, :] * branch, axis=1, keepdims=True)
    small[...] = jnp.where(lane == KS * KS + 1, scale_sum, small_in[...])


def pair_body(a, b, out):
    rows = a.shape[0]
    out[:rows, :] = a[...]
    out[rows:, :] = b[...]


def two_pairs_body(a, b, c, d, one, two):
    pair_body(a, b, one)
    pair_body(c, d, two)


def pair_of(a, b, after=None):
    return call(pair_body, [((2 * a.shape[0], a.shape[1]), F32)], [a, b], after=after)[0]


def gather_blocks(block, after=None):
    far = swap(block, "fsdp", 8)
    near_pair = pair_of(block, swap(block, "fsdp", 2), after)
    far_pair = pair_of(far, swap(far, "fsdp", 6), after)
    parts = [near_pair, swap(near_pair, "fsdp", 6), far_pair, swap(far_pair, "fsdp", 2)]
    return parts + [swap(part, "fsdp", 1) for part in parts]


class BlockScatter:
    def __init__(self, keep, send, first):
        self.keep, self.send = keep, send
        self.steps = [(4, 1), (2, first), (1, 8 - first)]

    def step(self, after=None):
        blocks, mask = self.steps.pop(0)
        of = ((blocks * BLK + EXT, SPOTS), F32)
        ins = [self.keep, swap(self.send, "fsdp", mask)]
        self.keep, self.send = call(half_sum_body, [of, of], ins, after=after)
        return self.send

    def last(self):
        return self.keep, swap(self.send, "fsdp", 8)


def shards(views, view_moves, grad_out, kernel, norm_gain, w_up, bias_up, w_down, layer_scale):
    one_map = (BLK, SPOTS)
    whole_map = (C, SPOTS)
    hid_map = (HID, SPOTS)
    cot = grad_out
    scale_row = layer_scale.reshape(1, BLK)
    gain_row = norm_gain.reshape(1, BLK)

    head, tail, picks = pl.pallas_call(
        start_body,
        out_shape=[
            jax.ShapeDtypeStruct((BLK, PIX), F32),
            jax.ShapeDtypeStruct((BLK, PIX), F32),
            jax.ShapeDtypeStruct((8,), jnp.int32),
        ],
        in_specs=[pl.BlockSpec(memory_space=pltpu.SMEM), pl.BlockSpec(memory_space=pltpu.VMEM)],
        out_specs=[pl.BlockSpec(memory_space=pltpu.VMEM)] * 2 + [pl.BlockSpec(memory_space=pltpu.SMEM)],
    )(view_moves, views)
    scot_own = call(
        scaled_body, [((BLK + EXT, SPOTS), F32)], [cot, scale_row, gain_row], after=tail
    )[0]
    next_view = shifted(head, "dp", -1)
    prior_view = shifted(tail, "dp", 1)
    flat, tall = (HID, C), (C, HID)
    token = ((8, 128), F32)
    *first_weights, ready = call(
        first_weights_body, [(flat, BF16)] * 4 + [token], [w_up, w_down], after=scot_own
    )
    placed, conv = call(
        forward_body,
        [(one_map, F32)] * 2,
        [picks, views, prior_view, next_view, kernel],
        smem=(0,),
        after=ready,
    )
    scot = gather_blocks(scot_own, conv)
    u_rows, u_rows_low, d_rows, d_rows_low, ready = call(
        second_weights_body,
        [(tall, BF16)] * 4 + [token],
        [w_up, w_down],
        scratch=[pltpu.VMEM(tall, F32)],
        after=conv,
    )
    conv_all = gather_blocks(conv, ready)
    bias = jnp.broadcast_to(bias_up[:, None], (HID, 128))
    u_high, u_low, d_high, d_low = first_weights
    s_high, s_low, gains, gain_up, d_hidden = call(
        cot_body,
        [(whole_map, BF16), (whole_map, BF16), ((C, 128), F32), ((HID, 128), F32), (hid_map, F32)],
        scot + [d_high, d_low, u_high, u_low],
        scratch=[pltpu.VMEM((C, 128), BF16)] * 2,
        after=ready,
    )
    outs = call(
        up_body,
        [((2 * BLK, C), F32)] + [((BLK, C), F32)] * 2
        + [(hid_map, BF16)] * 4
        + [(whole_map, BF16)] * 2
        + [((EXT, SPOTS), F32)] * 2
        + [((HID, 128), F32)],
        conv_all + [gains, u_high, u_low, bias, gain_up, s_high, s_low, d_hidden],
        scratch=[pltpu.VMEM(hid_map, F32)] + [pltpu.VMEM(hid_map, BF16)] * 2,
            )
    gd, (h_high, h_low, p_high, p_low, n_high, n_low, stats, sums, d_bias) = outs[:3], outs[3:]
    gu = call(
        grad_up_body,
        [((2 * HID, HID), F32)] + [((HID, HID), F32)] * 2,
        [n_high, n_low, p_high, p_low],
        us=3,
    )
    wide = [((8 * BLK + EXT, SPOTS), F32)] * 2
    norm_mine, norm_other = call(spread_body, wide, [u_rows, u_rows_low, p_high, p_low, sums], after=gu[0], us=3)
    branch_mine, branch_other = call(
        spread_body, wide, [d_rows, d_rows_low, h_high, h_low, sums], after=norm_mine, us=3
    )
    down, up = GroupSum(*gd), GroupSum(*gu)
    norm = BlockScatter(norm_mine, norm_other, 6)
    branch = BlockScatter(branch_mine, branch_other, 6)
    down.y_sum()
    up.y_sum()
    down.z_cut(after=norm.step())
    up.z_cut(after=branch.step())
    down.z_sum()
    up.z_sum()
    down.z_pair(after=norm.step())
    up.z_pair(after=branch.step())
    down.z_join(after=norm.step())
    up.z_join(after=branch.step())
    ready = down.y_pair()
    ready = up.y_pair(after=ready)
    d_placed, small = call(
        back_body,
        [((VG, BLK, PIX), F32), ((BLK, 128), F32)],
        [*norm.last(), stats, conv, placed, cot, kernel, gain_row],
        after=ready,
        us=8,
    )
    live, to_left, to_right, from_left, from_right = (picks[i] for i in range(2, 7))
    from_above = shifted(jnp.where(from_left > 0, d_placed[0], 0.0), "dp", -1)
    from_below = shifted(jnp.where(from_right > 0, d_placed[VG - 1], 0.0), "dp", 1)
    mixed, small = call(
        mixed_body,
        [((BLK, VG, PIX), F32), ((BLK, 128), F32)],
        [*branch.last(), placed, cot, scale_row, small],
    )
    small = jnp.concatenate([small, d_bias[:, 0].reshape(3, 128), jnp.zeros((5, 128), F32)], axis=0)
    for mask in (1, 2, 4, 8):
        small = small + swap(small, "dp", mask)
    grad_down = down.y_join(after=(from_above, from_below))
    grad_up = up.y_join(after=small)
    taps = KS * KS
    grad_kernel = small[:BLK, :taps]
    grad_gain = small[:BLK, taps]
    grad_scale = small[:BLK, taps + 1]
    grad_bias = small[BLK : BLK + 3].reshape(HID)

    slot_ids = jnp.arange(SLOTS, dtype=jnp.int32)[:, None, None]
    grad_views = jnp.zeros((SLOTS, BLK, PIX), F32)
    for j in range(VG):
        grad_views = jnp.where(slot_ids == picks[j] - CAP, d_placed[j][None], grad_views)
    grad_views = jnp.where((slot_ids == 0) & (to_left > 0), from_below[None], grad_views)
    grad_views = jnp.where((slot_ids == live - 1) & (to_right > 0), from_above[None], grad_views)
    grad_views = jnp.transpose(grad_views, (1, 0, 2))
    return (mixed, grad_views, grad_kernel, grad_gain, grad_up, grad_bias, grad_down, grad_scale)


def solution(mesh):
    return jax.shard_map(
        shards,
        mesh=mesh,
        in_specs=(
            P("fsdp", "dp", None),
            P(),
            P("fsdp", "dp", None),
            P("fsdp", None),
            P("fsdp"),
            P(None, "fsdp"),
            P("fsdp"),
            P("fsdp", None),
            P("fsdp"),
        ),
        out_specs=(
            P("fsdp", "dp", None),
            P("fsdp", "dp", None),
            P("fsdp", None),
            P("fsdp"),
            P(None, "fsdp"),
            P("fsdp"),
            P("fsdp", None),
            P("fsdp"),
        ),
        check_vma=False,
    )
```

```python
import functools

import jax
import jax.numpy as jnp
from jax import lax
from jax.experimental import pallas as pl
from jax.experimental.pallas import tpu as pltpu
from jax.sharding import PartitionSpec as P

C = 1536
HID = 384
SIDE = 16
KS = 7
REACH = KS // 2
VG = 2
CAP = 1
SLOTS = 4
PIX = SIDE * SIDE
SPOTS = VG * PIX
BLK = 96
EXT = 8
GROUPS = 16

EPSILON = 1e-06
ROOT_HALF = 0.7071067811865476
GAUSS_NORM = 0.3989422804014327
F32 = jnp.float32
BF16 = jnp.bfloat16

NEAR = ((0, 2), (6, 4))
FAR = ((8, 14), (10, 12))
GROUPED = NEAR + FAR + tuple((a ^ 1, b ^ 1) for a, b in NEAR + FAR)
SCATTER = {first: (0, 8, 8 - first, 16 - first, first, 8 + first, 4, 12) for first in (2, 6)}


def call(body, outs, ins, scratch=(), smem=(), after=None, us=1):
    after = [] if after is None else list(after) if isinstance(after, tuple) else [after]
    count = len(ins)
    if after:
        inner = body
        body = lambda *refs: inner(*refs[:count], *refs[count + len(after) :])
        ins = list(ins) + after
    shapes = [jax.ShapeDtypeStruct(s, d) for s, d in outs]
    spec = pl.BlockSpec(memory_space=pltpu.VMEM)
    return pl.pallas_call(
        body,
        out_shape=shapes,
        in_specs=[
            pl.BlockSpec(memory_space=pltpu.SMEM)
            if i in smem
            else pl.BlockSpec(memory_space=pl.ANY)
            if i >= count
            else spec
            for i in range(len(ins))
        ],
        out_specs=[spec] * len(outs),
        scratch_shapes=list(scratch),
        compiler_params=pltpu.CompilerParams(vmem_limit_bytes=40 * 2**20),
        cost_estimate=pl.CostEstimate(flops=us * 10**10, bytes_accessed=1024, transcendentals=0),
    )(*ins)


def swap(value, axis, mask):
    count = lax.axis_size(axis)
    return lax.ppermute(value, axis, [(i, i ^ mask) for i in range(count)])


def shifted(value, axis, steps):
    count = lax.axis_size(axis)
    leading, last = (max(0, -steps), min(count, count - steps))
    return lax.ppermute(value, axis, [(source, source + steps) for source in range(leading, last)])


def halves(value):
    high = value.astype(BF16)
    return high, (value - high.astype(F32)).astype(BF16)


def split_rows(source, high, low, first, count, target, chunk=32):
    def step(i, _):
        take = pl.ds(pl.multiple_of(first + i * chunk, chunk), chunk)
        put = pl.ds(pl.multiple_of(target + i * chunk, chunk), chunk)
        high[put, :], low[put, :] = halves(source[take, :])
        return 0

    lax.fori_loop(0, count // chunk, step, 0)


def product(a_high, a_low, b_high, b_low, contract):
    dims = (contract, ((), ()))
    dot = functools.partial(lax.dot_general, dimension_numbers=dims, preferred_element_type=F32)
    return dot(a_high, b_high) + dot(a_high, b_low) + dot(a_low, b_high)


NN = ((1,), (0,))
NT = ((1,), (1,))


def as_column(row):
    at = lax.broadcasted_iota(jnp.int32, (BLK, BLK), 0)
    to = lax.broadcasted_iota(jnp.int32, (BLK, BLK), 1)
    return jnp.sum(jnp.where(at == to, jnp.broadcast_to(row, (BLK, BLK)), 0.0), axis=1, keepdims=True)


def start_body(moves, views, head, tail, picks):
    g = lax.axis_index("dp")
    below = jnp.maximum(g - 1, 0)
    above = jnp.minimum(g + 1, GROUPS - 1)
    to_left = moves[g, 0]
    to_right = moves[g, 1]
    from_left = jnp.where(g > 0, moves[below, 1], 0)
    from_right = jnp.where(g < GROUPS - 1, moves[above, 0], 0)
    live = VG + to_left + to_right - from_left - from_right
    kept = live - to_left - to_right
    for j in range(VG):
        picks[j] = jnp.where(
            j < from_left,
            CAP - from_left + j,
            jnp.where(
                j < from_left + kept,
                CAP + to_left + j - from_left,
                CAP + SLOTS + j - from_left - kept,
            ),
        )
    picks[2] = live
    picks[3] = to_left
    picks[4] = to_right
    picks[5] = from_left
    picks[6] = from_right
    picks[7] = 0
    head[...] = views[:, 0, :]
    for s in range(SLOTS):

        @pl.when(jnp.maximum(live - 1, 0) == s)
        def _(s=s):
            tail[...] = views[:, s, :]


def scaled_body(cot, scale, gain, scot):
    column = as_column(scale[...])
    for v in range(VG):
        scot[0:BLK, v * PIX : (v + 1) * PIX] = cot[:, v, :] * column
    scot[BLK : BLK + EXT, :] = jnp.zeros((EXT, SPOTS), F32)
    scot[BLK : BLK + 1, 0:BLK] = gain[...]


def lane_place():
    lane = lax.broadcasted_iota(jnp.int32, (8, PIX), 1)
    return lane // SIDE, lane % SIDE


def moved(value, by, unit, where):
    if by == 0:
        return value
    rolled = pltpu.roll(value, (-by * unit) % PIX, 1)
    inside = (where + by >= 0) & (where + by < SIDE)
    return jnp.where(inside, rolled, 0.0)


def forward_body(picks, views, prior, after, kernel, placed, conv):
    def one(j, pick):
        spot = slice(j * PIX, (j + 1) * PIX)

        @pl.when(pick == 0)
        def _():
            placed[:, spot] = prior[...]

        @pl.when(pick == SLOTS + 1)
        def _():
            placed[:, spot] = after[...]

        for s in range(SLOTS):

            @pl.when(pick == CAP + s)
            def _(s=s):
                placed[:, spot] = views[:, s, :]

    for j in range(VG):
        one(j, picks[j])
    row, col = lane_place()

    def step(i, _):
        at = pl.ds(pl.multiple_of(i * 8, 8), 8)
        taps = kernel[at, :]
        maps = [placed[at, v * PIX : (v + 1) * PIX] for v in range(VG)]
        total = [jnp.zeros((8, PIX), F32) for _ in range(VG)]
        wide = [[moved(m, b - REACH, 1, col) for b in range(KS)] for m in maps]
        for a in range(KS):
            weights = [jnp.broadcast_to(taps[:, a * KS + b : a * KS + b + 1], (8, PIX)) for b in range(KS)]
            for v in range(VG):
                line = weights[0] * wide[v][0]
                for b in range(1, KS):
                    line = line + weights[b] * wide[v][b]
                total[v] = total[v] + moved(line, a - REACH, SIDE, row)
        for v in range(VG):
            conv[at, v * PIX : (v + 1) * PIX] = total[v]
        return 0

    lax.fori_loop(0, BLK // 8, step, 0)


def first_weights_body(w_up, w_down, u_high, u_low, d_high, d_low, done):
    def step(i, _):
        at = pl.ds(pl.multiple_of(i * 128, 128), 128)
        u_high[:, at], u_low[:, at] = halves(w_up[at, :].T)
        return 0

    lax.fori_loop(0, C // 128, step, 0)
    split_rows(w_down, d_high, d_low, 0, HID, 0)
    done[...] = jnp.zeros((8, 128), F32)


def second_weights_body(w_up, w_down, u_high, u_low, d_high, d_low, done, turned):
    f = lax.axis_index("fsdp")

    def step(i, _):
        at = pl.ds(pl.multiple_of(i * 128, 128), 128)
        turned[at, :] = w_down[:, at].T
        return 0

    lax.fori_loop(0, C // 128, step, 0)
    for source, high, low, first in ((w_up, u_high, u_low, 6), (turned, d_high, d_low, 6)):
        order = SCATTER[first]
        for q, m in enumerate(order + tuple(m ^ 1 for m in order)):
            split_rows(source, high, low, (f ^ m) * BLK, BLK, q * BLK)
    done[...] = jnp.zeros((8, 128), F32)


def cot_body(*refs):
    parts, refs = refs[:8], refs[8:]
    d_high, d_low, u_high, u_low, s_high, s_low, gains, gain_up, d_hidden, g_high, g_low = refs
    f = lax.axis_index("fsdp")
    for part, masks in zip(parts, GROUPED):
        for q, m in enumerate(masks):
            first = q * (BLK + EXT)
            at = pl.ds(pl.multiple_of((f ^ m) * BLK, 32), BLK)
            s_high[at, :], s_low[at, :] = halves(part[first : first + BLK, :])
            column = as_column(part[first + BLK : first + BLK + 1, 0:BLK])
            gains[at, :] = jnp.broadcast_to(column, (BLK, 128))
    def tile(n, _):
        at = pl.ds(pl.multiple_of(n * 256, 256), 256)
        d_hidden[:, at] = product(d_high[...], d_low[...], s_high[:, at], s_low[:, at], NN)
        return 0

    lax.fori_loop(0, SPOTS // 256, tile, 0)
    split_rows(gains, g_high, g_low, 0, C, 0)
    gain_up[...] = product(u_high[...], u_low[...], g_high[...], g_low[...], NN)


def up_body(*refs):
    parts, refs = refs[:8], refs[8:]
    gains, u_high, u_low, bias, gain_up, s_high, s_low, d_hidden = refs[:8]
    keep, send_a, send_b, h_high, h_low, p_high, p_low, n_high, n_low, stats, sums, d_bias = refs[8:20]
    up, y_high, y_low = refs[20:]
    f = lax.axis_index("fsdp")
    y = lax.axis_index("dp") % 4
    centre = sum(jnp.sum(part[...], axis=0, keepdims=True) for part in parts) / C
    spread = sum(jnp.sum((part[...] - centre) ** 2, axis=0, keepdims=True) for part in parts) / C
    inv_std = lax.rsqrt(spread + EPSILON)
    stats[...] = jnp.zeros((EXT, SPOTS), F32)
    stats[0:1, :] = centre
    stats[1:2, :] = inv_std
    for part, masks in zip(parts, GROUPED):
        for q, m in enumerate(masks):

            def piece(i, _, part=part, q=q, m=m):
                take = pl.ds(pl.multiple_of(q * BLK + i * 32, 32), 32)
                put = pl.ds(pl.multiple_of((f ^ m) * BLK + i * 32, 32), 32)
                gain = gains[put, :]
                value = (part[take, :] - centre) * inv_std * jnp.concatenate([gain] * 4, axis=1)
                n_high[put, :], n_low[put, :] = halves(value)
                return 0

            lax.fori_loop(0, BLK // 32, piece, 0)

    def tile(n, _):
        at = pl.ds(pl.multiple_of(n * 256, 256), 256)
        up[:, at] = product(u_high[...], u_low[...], n_high[:, at], n_low[:, at], NN)
        return 0

    lax.fori_loop(0, SPOTS // 256, tile, 0)

    def gelu(i, total):
        at = pl.ds(pl.multiple_of(i * 32, 32), 32)
        raw = up[at, :]
        pre = raw + jnp.concatenate([bias[at, :]] * 4, axis=1)
        cum = 0.5 * (1.0 + lax.erf(pre * ROOT_HALF))
        hidden = pre * cum
        slope = cum + pre * jnp.exp(-0.5 * pre * pre) * GAUSS_NORM
        d_pre = d_hidden[at, :] * slope
        high, low = halves(hidden)
        h_high[at, :], h_low[at, :] = high, low
        put = pl.ds(pl.multiple_of(((i // 3) ^ y) * BLK + (i % 3) * 32, 32), 32)
        y_high[put, :], y_low[put, :] = high, low
        p_high[at, :], p_low[at, :] = halves(d_pre)
        d_bias[at, :] = jnp.broadcast_to(jnp.sum(d_pre, axis=1, keepdims=True), (32, 128))
        plain = jnp.sum(d_pre * jnp.concatenate([gain_up[at, :]] * 4, axis=1), axis=0, keepdims=True)
        cross = jnp.sum(d_pre * raw, axis=0, keepdims=True)
        return total[0] + plain, total[1] + cross

    zero = jnp.zeros((1, SPOTS), F32)
    plain, cross = lax.fori_loop(0, HID // 32, gelu, (zero, zero))
    sums[...] = jnp.zeros((EXT, SPOTS), F32)
    sums[0:1, :] = plain
    sums[1:2, :] = cross

    def down(n, _):
        at = pl.ds(pl.multiple_of(n * 256, 256), 256)
        got = product(y_high[...], y_low[...], s_high[at, :], s_low[at, :], NT)
        for k in range(4):
            lay_out(k, got[k * BLK : (k + 1) * BLK, :], keep, send_a, send_b, at)
        return 0

    lax.fori_loop(0, C // 256, down, 0)


def grad_up_body(n_high, n_low, p_high, p_low, keep, send_a, send_b):
    y = lax.axis_index("dp") % 4
    for k in range(4):
        at = pl.ds(pl.multiple_of((y ^ k) * HID, HID), HID)
        got = product(n_high[at, :], n_low[at, :], p_high[...], p_low[...], NT)
        lay_out(k, got, keep, send_a, send_b, slice(None))


def spread_body(a_high, a_low, b_high, b_low, sums, mine, other):
    for out, flip in ((other, 1), (mine, 0)):
        rows = slice(flip * 8 * BLK, (flip + 1) * 8 * BLK)

        def tile(n, _, out=out, rows=rows):
            at = pl.ds(pl.multiple_of(n * 256, 256), 256)
            high, low = a_high[rows, :], a_low[rows, :]
            out[0 : 8 * BLK, at] = product(high, low, b_high[:, at], b_low[:, at], NN)
            return 0

        lax.fori_loop(0, SPOTS // 256, tile, 0)
        out[8 * BLK : 8 * BLK + EXT, :] = sums[...]


def half_sum_body(a, b, keep, send):
    rows = keep.shape[0] - EXT
    sums = a[2 * rows :, :] + b[2 * rows :, :]
    for k, out in enumerate((keep, send)):
        at = slice(rows * k, rows * (k + 1))
        out[0:rows, :] = a[at, :] + b[at, :]
        out[rows : rows + EXT, :] = sums


def lay_out(k, value, keep, send_a, send_b, at):
    half = value.shape[0] // 2
    a_to, a_place = ((keep, 0), (send_a, 0), (send_a, 1), (keep, 1))[k]
    b_to, b_place = ((keep, 2), (keep, 3), (send_b, 1), (send_b, 0))[k]
    a_to[a_place * half : (a_place + 1) * half, at] = value[:half]
    b_to[b_place * half : (b_place + 1) * half, at] = value[half:]


def y_sum_body(keep, got_a, got_b, own, send_a, send_b):
    half = send_a.shape[0]
    one, two, three, four = (slice(half * i, half * (i + 1)) for i in range(4))
    own[one, :] = keep[one, :] + got_a[one, :]
    send_a[...] = keep[two, :] + got_a[two, :]
    own[two, :] = keep[three, :] + got_b[one, :]
    send_b[...] = keep[four, :] + got_b[two, :]


def z_cut_body(own, got_a, got_b, keep, send, piece):
    z = lax.axis_index("dp") // 4
    half = got_a.shape[0]
    rows = half // 2
    piece[:half, :] = own[:half, :] + got_a[...]
    piece[half:, :] = own[half:, :] + got_b[...]
    for out, pair in ((keep, (0, 2)), (send, (1, 3))):
        for i, q in enumerate(pair):
            out[i * rows : (i + 1) * rows, :] = piece[pl.ds(pl.multiple_of((z ^ q) * rows, 8), rows), :]


def z_sum_body(keep, got, own, send):
    rows = own.shape[0]
    own[...] = keep[:rows, :] + got[:rows, :]
    send[...] = keep[rows:, :] + got[rows:, :]


def z_join_body(pair, got, part_a, part_b, piece):
    z = lax.axis_index("dp") // 4
    half = part_a.shape[0]
    rows = half // 2
    for source, order in ((pair, (0, 2)), (got, (1, 3))):
        for i, q in enumerate(order):
            piece[pl.ds(pl.multiple_of((z ^ q) * rows, 8), rows), :] = source[i * rows : (i + 1) * rows, :]
    part_a[...] = piece[:half, :]
    part_b[...] = piece[half:, :]


def y_join_body(have_a, have_b, got_a, got_b, out):
    y = lax.axis_index("dp") % 4
    half = have_a.shape[0] // 2
    for source, which, order in ((have_a, 0, (0, 3)), (got_a, 0, (1, 2)), (have_b, 1, (0, 1)), (got_b, 1, (3, 2))):
        for i, k in enumerate(order):
            at = pl.ds(pl.multiple_of((y ^ k) * 2 * half + which * half, 8), half)
            out[at, :] = source[i * half : (i + 1) * half, :]


class GroupSum:
    def __init__(self, keep, send_a, send_b):
        self.half, self.columns = keep.shape[0] // 4, keep.shape[1]
        self.piece = [pltpu.VMEM((2 * self.half, self.columns), F32)]
        self.keep, self.send = keep, (send_a, send_b)

    def of(self, count):
        return ((count, self.columns), F32)

    def y_sum(self, after=None):
        ins = [self.keep, swap(self.send[0], "dp", 1), swap(self.send[1], "dp", 3)]
        outs = [self.of(2 * self.half), self.of(self.half), self.of(self.half)]
        self.keep, *self.send = call(y_sum_body, outs, ins, after=after)
        return self.keep

    def z_cut(self, after=None):
        ins = [self.keep, swap(self.send[0], "dp", 3), swap(self.send[1], "dp", 1)]
        outs = [self.of(self.half)] * 2
        self.keep, self.send = call(z_cut_body, outs, ins, scratch=self.piece, after=after)
        return self.keep

    def z_sum(self, after=None):
        ins = [self.keep, swap(self.send, "dp", 4)]
        outs = [self.of(self.half // 2)] * 2
        self.keep, self.send = call(z_sum_body, outs, ins, after=after)
        return self.keep

    def z_pair(self, after=None):
        own = self.keep + swap(self.send, "dp", 8)
        self.pair = pair_of(own, swap(own, "dp", 8), after)
        return self.pair

    def z_join(self, after=None):
        ins = [self.pair, swap(self.pair, "dp", 4)]
        outs = [self.of(self.half)] * 2
        self.parts = call(z_join_body, outs, ins, scratch=self.piece, after=after)
        return self.parts[0]

    def y_pair(self, after=None):
        one, two = self.parts
        ins = [one, swap(one, "dp", 3), two, swap(two, "dp", 1)]
        self.have = call(two_pairs_body, [self.of(2 * self.half)] * 2, ins, after=after)
        return self.have[1]

    def y_join(self, after=None):
        one, two = self.have
        ins = [one, two, swap(one, "dp", 1), swap(two, "dp", 3)]
        return call(y_join_body, [self.of(8 * self.half)], ins, after=after)[0]


def back_body(keep, got, stats, conv, placed, cot, kernel, gain, d_placed, small):
    centre, inv_std = stats[0:1, :], stats[1:2, :]
    mean_q = (keep[BLK : BLK + 1, :] + got[BLK : BLK + 1, :]) / C
    cross = slice(BLK + 1, BLK + 2)
    mean_cross = (keep[cross, :] + got[cross, :]) / C
    small[...] = jnp.broadcast_to(as_column(gain[...]), (BLK, 128))
    row, col = lane_place()
    lane = lax.broadcasted_iota(jnp.int32, (8, 128), 1)

    def step(i, _):
        at = pl.ds(pl.multiple_of(i * 8, 8), 8)
        taps = kernel[at, :]
        d_normed = keep[at, :] + got[at, :]
        standard = (conv[at, :] - centre) * inv_std
        gains = jnp.concatenate([small[at, :]] * 4, axis=1)
        d_conv = inv_std * (d_normed * gains - mean_q - standard * mean_cross)
        packed = jnp.where(
            lane == KS * KS, jnp.sum(d_normed * standard, axis=1, keepdims=True), 0.0
        )
        partial = {}
        for v in range(VG):
            spot = slice(v * PIX, (v + 1) * PIX)
            delta = d_conv[:, spot]
            maps = placed[at, spot]
            wide_d = [moved(delta, REACH - b, 1, col) for b in range(KS)]
            wide_x = [moved(maps, b - REACH, 1, col) for b in range(KS)]
            total = cot[at, v, :]
            for a in range(KS):
                line = jnp.zeros((8, PIX), F32)
                tall = moved(delta, REACH - a, SIDE, row)
                for b in range(KS):
                    t = a * KS + b
                    line = line + taps[:, t : t + 1] * wide_d[b]
                    term = tall * wide_x[b]
                    term = term[:, :128] + term[:, 128:]
                    partial[t] = term if v == 0 else partial[t] + term
                total = total + moved(line, REACH - a, SIDE, row)
            d_placed[v, at, :] = total
        for t in range(KS * KS):
            packed = jnp.where(lane == t, jnp.sum(partial[t], axis=1, keepdims=True), packed)
        small[at, :] = packed
        return 0

    lax.fori_loop(0, BLK // 8, step, 0)


def mixed_body(keep, got, placed, cot, scale, small_in, mixed, small):
    column = as_column(scale[...])
    lane = lax.broadcasted_iota(jnp.int32, (BLK, 128), 1)
    scale_sum = jnp.zeros((BLK, 1), F32)
    for v in range(VG):
        spot = slice(v * PIX, (v + 1) * PIX)
        branch = keep[0:BLK, spot] + got[0:BLK, spot]
        mixed[:, v, :] = placed[:, spot] + column * branch
        scale_sum = scale_sum + jnp.sum(cot[:, v, :] * branch, axis=1, keepdims=True)
    small[...] = jnp.where(lane == KS * KS + 1, scale_sum, small_in[...])


def pair_body(a, b, out):
    rows = a.shape[0]
    out[:rows, :] = a[...]
    out[rows:, :] = b[...]


def two_pairs_body(a, b, c, d, one, two):
    pair_body(a, b, one)
    pair_body(c, d, two)


def pair_of(a, b, after=None, us=1):
    return call(pair_body, [((2 * a.shape[0], a.shape[1]), F32)], [a, b], after=after, us=us)[0]


def gather_blocks(block, after=None):
    far = swap(block, "fsdp", 8)
    near_pair = pair_of(block, swap(block, "fsdp", 2), after, us=0)
    far_pair = pair_of(far, swap(far, "fsdp", 6), after, us=0)
    parts = [near_pair, swap(near_pair, "fsdp", 6), far_pair, swap(far_pair, "fsdp", 2)]
    return parts + [swap(part, "fsdp", 1) for part in parts]


class BlockScatter:
    def __init__(self, keep, send, first):
        self.keep, self.send = keep, send
        self.steps = [(4, 1), (2, first), (1, 8 - first)]

    def step(self, after=None):
        blocks, mask = self.steps.pop(0)
        of = ((blocks * BLK + EXT, SPOTS), F32)
        ins = [self.keep, swap(self.send, "fsdp", mask)]
        self.keep, self.send = call(half_sum_body, [of, of], ins, after=after)
        return self.send

    def last(self):
        return self.keep, swap(self.send, "fsdp", 8)


def shards(views, view_moves, grad_out, kernel, norm_gain, w_up, bias_up, w_down, layer_scale):
    one_map = (BLK, SPOTS)
    whole_map = (C, SPOTS)
    hid_map = (HID, SPOTS)
    cot = grad_out
    scale_row = layer_scale.reshape(1, BLK)
    gain_row = norm_gain.reshape(1, BLK)

    head, tail, picks = pl.pallas_call(
        start_body,
        out_shape=[
            jax.ShapeDtypeStruct((BLK, PIX), F32),
            jax.ShapeDtypeStruct((BLK, PIX), F32),
            jax.ShapeDtypeStruct((8,), jnp.int32),
        ],
        in_specs=[pl.BlockSpec(memory_space=pltpu.SMEM), pl.BlockSpec(memory_space=pltpu.VMEM)],
        out_specs=[pl.BlockSpec(memory_space=pltpu.VMEM)] * 2 + [pl.BlockSpec(memory_space=pltpu.SMEM)],
    )(view_moves, views)
    scot_own = call(
        scaled_body, [((BLK + EXT, SPOTS), F32)], [cot, scale_row, gain_row], after=tail, us=0
    )[0]
    next_view = shifted(head, "dp", -1)
    prior_view = shifted(tail, "dp", 1)
    flat, tall = (HID, C), (C, HID)
    token = ((8, 128), F32)
    *first_weights, ready = call(
        first_weights_body, [(flat, BF16)] * 4 + [token], [w_up, w_down], after=scot_own, us=0
    )
    placed, conv = call(
        forward_body,
        [(one_map, F32)] * 2,
        [picks, views, prior_view, next_view, kernel],
        smem=(0,),
        after=ready,
        us=0,
    )
    scot = gather_blocks(scot_own, conv)
    u_rows, u_rows_low, d_rows, d_rows_low, ready = call(
        second_weights_body,
        [(tall, BF16)] * 4 + [token],
        [w_up, w_down],
        scratch=[pltpu.VMEM(tall, F32)],
        after=conv,
        us=0,
    )
    conv_all = gather_blocks(conv, ready)
    bias = jnp.broadcast_to(bias_up[:, None], (HID, 128))
    u_high, u_low, d_high, d_low = first_weights
    s_high, s_low, gains, gain_up, d_hidden = call(
        cot_body,
        [(whole_map, BF16), (whole_map, BF16), ((C, 128), F32), ((HID, 128), F32), (hid_map, F32)],
        scot + [d_high, d_low, u_high, u_low],
        scratch=[pltpu.VMEM((C, 128), BF16)] * 2,
        us=0,
        after=ready,
    )
    outs = call(
        up_body,
        [((2 * BLK, C), F32)] + [((BLK, C), F32)] * 2
        + [(hid_map, BF16)] * 4
        + [(whole_map, BF16)] * 2
        + [((EXT, SPOTS), F32)] * 2
        + [((HID, 128), F32)],
        conv_all + [gains, u_high, u_low, bias, gain_up, s_high, s_low, d_hidden],
        scratch=[pltpu.VMEM(hid_map, F32)] + [pltpu.VMEM(hid_map, BF16)] * 2,
            )
    gd, (h_high, h_low, p_high, p_low, n_high, n_low, stats, sums, d_bias) = outs[:3], outs[3:]
    gu = call(
        grad_up_body,
        [((2 * HID, HID), F32)] + [((HID, HID), F32)] * 2,
        [n_high, n_low, p_high, p_low],
        us=3,
    )
    wide = [((8 * BLK + EXT, SPOTS), F32)] * 2
    norm_mine, norm_other = call(spread_body, wide, [u_rows, u_rows_low, p_high, p_low, sums], after=gu[0], us=3)
    branch_mine, branch_other = call(
        spread_body, wide, [d_rows, d_rows_low, h_high, h_low, sums], after=norm_mine, us=3
    )
    down, up = GroupSum(*gd), GroupSum(*gu)
    norm = BlockScatter(norm_mine, norm_other, 6)
    branch = BlockScatter(branch_mine, branch_other, 6)
    down.y_sum()
    up.y_sum()
    down.z_cut(after=norm.step())
    up.z_cut(after=branch.step())
    down.z_sum()
    up.z_sum()
    down.z_pair(after=norm.step())
    up.z_pair(after=branch.step())
    down.z_join(after=norm.step())
    up.z_join(after=branch.step())
    ready = down.y_pair()
    ready = up.y_pair(after=ready)
    d_placed, small = call(
        back_body,
        [((VG, BLK, PIX), F32), ((BLK, 128), F32)],
        [*norm.last(), stats, conv, placed, cot, kernel, gain_row],
        after=ready,
        us=8,
    )
    live, to_left, to_right, from_left, from_right = (picks[i] for i in range(2, 7))
    from_above = shifted(jnp.where(from_left > 0, d_placed[0], 0.0), "dp", -1)
    from_below = shifted(jnp.where(from_right > 0, d_placed[VG - 1], 0.0), "dp", 1)
    mixed, small = call(
        mixed_body,
        [((BLK, VG, PIX), F32), ((BLK, 128), F32)],
        [*branch.last(), placed, cot, scale_row, small],
    )
    small = jnp.concatenate([small, d_bias[:, 0].reshape(3, 128), jnp.zeros((5, 128), F32)], axis=0)
    for mask in (1, 2, 4, 8):
        small = small + swap(small, "dp", mask)
    grad_down = down.y_join(after=(from_above, from_below))
    grad_up = up.y_join(after=small)
    taps = KS * KS
    grad_kernel = small[:BLK, :taps]
    grad_gain = small[:BLK, taps]
    grad_scale = small[:BLK, taps + 1]
    grad_bias = small[BLK : BLK + 3].reshape(HID)

    slot_ids = jnp.arange(SLOTS, dtype=jnp.int32)[:, None, None]
    grad_views = jnp.zeros((SLOTS, BLK, PIX), F32)
    for j in range(VG):
        grad_views = jnp.where(slot_ids == picks[j] - CAP, d_placed[j][None], grad_views)
    grad_views = jnp.where((slot_ids == 0) & (to_left > 0), from_below[None], grad_views)
    grad_views = jnp.where((slot_ids == live - 1) & (to_right > 0), from_above[None], grad_views)
    grad_views = jnp.transpose(grad_views, (1, 0, 2))
    return (mixed, grad_views, grad_kernel, grad_gain, grad_up, grad_bias, grad_down, grad_scale)


def solution(mesh):
    return jax.shard_map(
        shards,
        mesh=mesh,
        in_specs=(
            P("fsdp", "dp", None),
            P(),
            P("fsdp", "dp", None),
            P("fsdp", None),
            P("fsdp"),
            P(None, "fsdp"),
            P("fsdp"),
            P("fsdp", None),
            P("fsdp"),
        ),
        out_specs=(
            P("fsdp", "dp", None),
            P("fsdp", "dp", None),
            P("fsdp", None),
            P("fsdp"),
            P(None, "fsdp"),
            P("fsdp"),
            P("fsdp", None),
            P("fsdp"),
        ),
        check_vma=False,
    )
```
